32 devices in a mesh: groups: 2 (over y), builds: 16 (over z, x, core).
Axes of the slice: x: 2, y: 2, z: 4, core: 2. Of those that a mesh axis runs over, the one named last changes fastest.
Arguments:
- build_factors: bfloat16 [393216, 256], P('builds')
- nz_build: int32 [16384], P(('groups', 'builds')), parts along dimension 0, may hold values from 0 to 24575
- nz_test: int32 [16384, 1], P(('groups', 'builds')), parts along dimension 0, may hold values from 0 to 255; in each aligned block of 512 rows (0 to 511, 512 to 1023, ...) at most 4 rows name the same one
- nz_count: int32 [16384], P(('groups', 'builds')), parts along dimension 0, may hold values from 1 to 15
- start_factors: float32 [512, 256], P(('groups', 'builds')), parts along dimension 0, may hold values from -6 to 6
Outputs:
- test_factors: float32 [512, 256], P(('groups', 'builds')), parts along dimension 0
The draws below stay inside these ranges and needn't reach their ends.
There are 2 independent parts, one for each index of `groups`. The reference program is written for one: setup_inputs(seed, part) draws one part's arguments, and reference() takes and returns one part's arrays. A program takes and returns all parts, laid end to end along the dimension named above; an argument that names none is the same for every part. Nothing has to cross between parts.
Inputs may be any that keep to these rules, and one draw needn't show every extreme that they name: `nz_test`: among the nonzeros of one device no test appears more than 4 times, and on every device some test appears exactly 4 times.
All inputs are finite; a program needn't handle non-finite values.
Results may differ from the reference program's by a relative error of at most 0.0003.
Values may be sent and summed in bfloat16 or wider, within the bound.
A program may use at most 64 MiB of HBM per device.

```python
import math
import jax
import jax.numpy as jnp
import numpy as np
from jax import lax

RANK = 256
BLD_DEV = 24576
TEST_DEV = 16
MOST = 4
ITERS = 3
BUILDS = 393216
TESTS = 256
NZ_DEV = 512
NZ = 8192
N_BUILDS = 16


def draw_build_factors(key, part):
    key = jax.random.fold_in(key, 7)
    key_base, key_rows, key_cols = jax.random.split(key, 3)
    half_range = 1.1513
    row_scale = jnp.exp(jax.random.uniform(key_rows, (BUILDS, 1), jnp.float32, -half_range, half_range))
    col_scale = jnp.exp(jax.random.uniform(key_cols, (1, RANK), jnp.float32, -half_range, half_range))
    position = jnp.arange(BUILDS, dtype=jnp.float32)[:, None] / BUILDS
    trend_scale = jnp.exp((position - 0.5) * 1.0986)
    base_vals = jax.random.normal(key_base, (BUILDS, RANK), jnp.float32)
    base_vals = jnp.clip(base_vals, -4.0, 4.0)
    spread = (TEST_DEV / NZ_DEV) ** 0.5
    return (base_vals * row_scale * trend_scale * col_scale * spread).astype(jnp.bfloat16)


def touch_ends(values, stream_key, low, largest):
    shape = values.shape
    index_at = [jax.random.randint(jax.random.fold_in(stream_key, axis), (), 0, shape[axis]) for axis in range(len(shape))]
    values = values.at[tuple(index_at)].set(low)
    longest = shape.index(max(shape))
    index_at[longest] = (index_at[longest] + 1) % shape[longest]
    return values.at[tuple(index_at)].set(largest)


def steps_of(rng, shape, pieces, least, high):
    gain, own = 1.0, jax.random.fold_in(rng, 6)
    for dim, blocks in pieces:
        draws = jnp.exp(jax.random.uniform(jax.random.fold_in(own, dim), (blocks,), jnp.float32, least / len(pieces), high / len(pieces)))
        gain = gain * jnp.repeat(draws, shape[dim] // blocks).reshape([-1 if axis == dim else 1 for axis in range(len(shape))])
    return gain


def assign_block(stream_key, own, number, rows, number_of, top, reach, skew):
    sequence = jax.random.permutation(stream_key, number_of)
    crowded, common = load_shares(number_of, rows * top, reach, skew, True), load_shares(number_of, rows * top, reach, skew, False)
    places = jnp.arange(number_of)

    def named(tallies, rotation):
        used = int((tallies > 0).sum())
        fixed = max(1, used // 4)
        moved = fixed + (places - fixed + rotation * (used - fixed)) % max(1, number_of - fixed)
        return jnp.zeros((number_of,), jnp.int32).at[sequence[jnp.where(places < fixed, places, moved)]].set(jnp.asarray(tallies, jnp.int32))

    tallies = jnp.where(number % 4 == 0, named(crowded, number // 4), named(common, number - number // 4 - 1))
    mixed = jax.random.permutation(jax.random.fold_in(own, 3), number_of)
    source_of, sink = mixed[0:number_of // 2 * 2:2], mixed[1:number_of // 2 * 2:2]
    room = jnp.minimum(tallies[source_of] - 1, reach - tallies[sink]) // 2
    room = jnp.where((source_of == sequence[0]) | (sink == sequence[0]) | (tallies[sink] == 0), 0, jnp.maximum(room, 0))
    moved = jax.random.randint(jax.random.fold_in(own, 4), (number_of // 2,), 0, 1 << 20) % (room + 1)
    tallies = tallies.at[source_of].add(-moved).at[sink].add(moved)
    labels = jnp.searchsorted(jnp.cumsum(tallies), jnp.arange(rows * top), side="right").astype(jnp.int32)
    grid = labels.reshape(top, rows).T
    grid = grid[jax.random.permutation(jax.random.fold_in(own, 1), rows)]
    rotation = jax.random.randint(jax.random.fold_in(own, 2), (rows, 1), 0, top)
    return jnp.take_along_axis(grid, (jnp.arange(top)[None, :] + rotation) % top, axis=1)


def load_shares(amount, total, limit, lean, full):
    loads = [(1 << 20) // math.isqrt(rank ** lean) + 1 for rank in range(1, amount + 1)]
    largest = limit if full else min(limit, max(-(-total // amount), total * loads[0] // sum(loads)))
    least = 1 if total - largest >= amount - 1 else 0
    counts, spare = [largest] + [least] * (amount - 1), total - largest - least * (amount - 1)
    while spare > 0:
        candidates = [i for i in range(1, amount) if counts[i] < largest] or [i for i in range(1, amount) if counts[i] < limit]
        whole, budget = sum([loads[i] for i in candidates]), spare
        for i in candidates:
            extra = min(limit - counts[i], max(1, budget * loads[i] // whole), spare)
            counts[i] = counts[i] + extra
            spare = spare - extra
    return np.array(counts)


def normal_values(key, shape, width, most, shards=(), kind=jnp.bfloat16):
    result = jax.random.normal(key, shape, jnp.float32) * width
    if len(shards) > 0:
        result = steps_of(key, shape, shards, -0.22, 0.18) * result
    return jnp.clip(result, min=-most, max=most).astype(kind)


def setup_inputs(seed: int = 0, part: int = 0) -> dict:
    streams_of = jax.random.split(jax.random.key(seed), 6)
    part_keys = jax.random.split(jax.random.fold_in(streams_of[5], part), 6)
    build_factors = draw_build_factors(jax.random.fold_in(streams_of[5], 71), part)
    nz_build = touch_ends(jax.random.randint(part_keys[1], (NZ,), 0, BLD_DEV), jax.random.fold_in(part_keys[1], 1), 0, BLD_DEV - 1).astype(jnp.int32)
    nz_test_keys = jax.random.split(jax.random.fold_in(part_keys[2], 1), NZ // NZ_DEV)
    nz_test_turns = jax.random.permutation(jax.random.fold_in(part_keys[2], 3), NZ // NZ_DEV)
    nz_test = jax.vmap(lambda own, number: assign_block(jax.random.fold_in(part_keys[2], 2), own, number, NZ_DEV, TESTS, 1, MOST, 2))(nz_test_keys, nz_test_turns).reshape((NZ, 1))
    nz_count = touch_ends(jax.random.randint(part_keys[3], (NZ,), 1, 16), jax.random.fold_in(part_keys[3], 1), 1, 15).astype(jnp.int32)
    start_factors = normal_values(part_keys[4], (TESTS, RANK), 1.0, 6.0, ((0, 16),), jnp.float32)
    return {"build_factors": build_factors, "nz_build": nz_build, "nz_test": nz_test, "nz_count": nz_count, "start_factors": start_factors}


epsilon = 1e-6


def reference(build_factors, nz_build, nz_test, nz_count, start_factors):
    conf_scale = BUILDS * TEST_DEV / (8.0 * NZ_DEV)
    damping = 0.4 * conf_scale
    row_blocks = build_factors.reshape(N_BUILDS, BLD_DEV, RANK)

    def add_gram(running, block_rows):
        wide_rows = block_rows.astype(jnp.float32)
        return running + jnp.dot(wide_rows.T, wide_rows, precision=lax.Precision.HIGHEST), None

    shared, unused = lax.scan(add_gram, jnp.zeros((RANK, RANK), jnp.float32), row_blocks)
    offsets = jnp.arange(N_BUILDS, dtype=jnp.int32) * BLD_DEV
    nz_blocks = (nz_build.reshape(N_BUILDS, NZ_DEV), nz_test[:, 0].reshape(N_BUILDS, NZ_DEV),
                 nz_count.reshape(N_BUILDS, NZ_DEV), offsets)

    def sparse_apply(factors, with_target):
        def add_block(running, block_item):
            local_rows, test_ids, count_vals, row_offset = block_item
            build_rows = build_factors[local_rows + row_offset].astype(jnp.float32)
            inner_vals = jnp.sum(build_rows * factors[test_ids], axis=1)
            weight = conf_scale * count_vals.astype(jnp.float32)
            coeffs = weight * (1.0 - inner_vals) if with_target else weight * inner_vals
            partial_value = jax.ops.segment_sum(coeffs[:, None] * build_rows, test_ids, num_segments=TESTS)
            return running + partial_value, None

        running, unused = lax.scan(add_block, jnp.zeros((TESTS, RANK), jnp.float32), nz_blocks)
        return running

    def dense_part(field):
        return jnp.dot(field, shared, precision=lax.Precision.HIGHEST) + damping * field

    factors = start_factors
    residual = sparse_apply(start_factors, True) - dense_part(start_factors)
    direction = residual
    norm_now = jnp.sum(residual * residual, axis=1)
    for sweep_idx in range(ITERS):
        image_vec = sparse_apply(direction, False) + dense_part(direction)
        step_size = norm_now / (jnp.sum(direction * image_vec, axis=1) + epsilon)
        factors = factors + step_size[:, None] * direction
        residual = residual - step_size[:, None] * image_vec
        norm_next = jnp.sum(residual * residual, axis=1)
        direction = residual + (norm_next / (norm_now + epsilon))[:, None] * direction
        norm_now = norm_next
    return factors
```

```python
import functools

import jax
import jax.numpy as jnp
from jax import lax
from jax.experimental import pallas as pl
from jax.experimental.pallas import tpu as pltpu
from jax.sharding import PartitionSpec as P

ITERS = 3
MOST = 4
epsilon = 1e-06
f32 = jnp.float32
bf16 = jnp.bfloat16


def pieces(v):
    high = v.astype(bf16)
    rest = v - high.astype(f32)
    mid = rest.astype(bf16)
    low = (rest - mid.astype(f32)).astype(bf16)
    return jnp.concatenate([high, mid, low], axis=0)


def add_pieces(v):
    rows = v.shape[0] // 3
    return v[:rows] + v[rows : 2 * rows] + v[2 * rows :]


def nt(a, b):
    return lax.dot_general(a, b, (((1,), (1,)), ((), ())), preferred_element_type=f32)


def tn(a, b):
    return lax.dot_general(a, b, (((0,), (0,)), ((), ())), preferred_element_type=f32)


def kernel(
    n, owners, conf_scale, damping,
    x_hbm, picked, slot, count, start, out,
    x_buf, gram, tri, tri_in, tri_sum, y_out, y_in, w_out, w_in,
    x_sem, y_send, y_recv, w_send, w_recv, g_send, g_recv, s_send, s_recv,
):
    me = lax.axis_index("builds")
    chunks, chunk, _ = x_buf.shape
    tests = start.shape[0]
    slots = tests * MOST
    width = w_out.shape[2]
    part = tri.shape[1]
    half = tri.shape[2]

    def load(c):
        return pltpu.make_async_copy(
            x_hbm.at[pl.ds(pl.multiple_of(c * chunk, chunk), chunk), :], x_buf.at[c], x_sem.at[c]
        )

    @pl.loop(0, chunks)
    def _(c):
        load(c).start()

    barrier = pltpu.get_barrier_semaphore()

    @pl.loop(1, n)
    def _(j):
        pl.semaphore_signal(
            barrier, inc=1, device_id={"builds": lax.rem(me + j, n)}, device_id_type=pl.DeviceIdType.MESH
        )

    def remote(src, dst, send, recv, to):
        return pltpu.make_async_remote_copy(
            src_ref=src, dst_ref=dst, send_sem=send, recv_sem=recv,
            device_id={"builds": to}, device_id_type=pl.DeviceIdType.MESH,
        )

    def y_copy(to, source):
        return remote(y_out.at[to], y_in.at[source], y_send.at[to], y_recv.at[source], to)

    def w_copy(to, source):
        return remote(w_out.at[to], w_in.at[source], w_send.at[to], w_recv.at[source], to)

    def block_of(owner):
        local = slot[...] - owner * slots
        local = jnp.where((local >= 0) & (local < slots), local, -1)
        row = lax.broadcasted_iota(jnp.int32, (width, local.shape[1]), 0)
        place = (row == local).astype(f32).astype(bf16)
        rows = jnp.dot(place[:slots], picked[...], preferred_element_type=f32).astype(bf16)
        counts = nt(count[...], place)
        test = lax.broadcasted_iota(jnp.int32, counts.shape, 0)
        lane = lax.broadcasted_iota(jnp.int32, counts.shape, 1)
        return rows, jnp.where(lane // MOST == test, counts, 0.0).astype(bf16)

    rows, counts = block_of(me)
    y_in[me] = rows
    w_in[me] = counts
    pl.semaphore_wait(barrier, n - 1)

    @pl.loop(1, n)
    def _(j):
        to = lax.rem(me + j, n)
        rows, counts = block_of(to)
        y_out[to] = rows
        w_out[to] = counts
        y_copy(to, me).start()
        w_copy(to, me).start()

    gram[...] = jnp.zeros_like(gram)

    @pl.loop(0, chunks)
    def _(c):
        load(c).wait()
        x = x_buf[c]
        gram[...] += tn(x, x)

    per = half // part
    for i in range(per):
        tri[i] = gram[i * part : (i + 1) * part, :half]
        tri[per + i] = gram[i * part : (i + 1) * part, half:]
        tri[2 * per + i] = gram[half + i * part : half + (i + 1) * part, half:]

    share = tri.shape[0] // owners

    def g_copy(to, source):
        return remote(
            tri.at[pl.ds(to * share, share)], tri_in.at[source], g_send.at[to], g_recv.at[source], to
        )

    def s_copy(to, source):
        tiles = pl.ds(source * share, share)
        return remote(tri_sum.at[tiles], tri_sum.at[tiles], s_send.at[to], s_recv.at[source], to)

    def each_owner(body):
        @pl.loop(1, n)
        def _(j):
            other = lax.rem(me + j, n)
            if owners == n:
                body(other)
            else:
                pl.when(other < owners)(lambda: body(other))

    def each_other(body):
        @pl.loop(1, n)
        def _(j):
            body(lax.rem(me + j, n))

    def if_owner(body):
        if owners == n:
            body()
        else:
            pl.when(me < owners)(body)

    each_owner(lambda to: g_copy(to, me).start())

    def reduce():
        tri_in[me] = tri[pl.ds(me * share, share)]
        each_other(lambda source: g_copy(me, source).wait_recv())
        tri_sum[pl.ds(me * share, share)] = jnp.sum(tri_in[...], axis=0)
        each_other(lambda to: s_copy(to, me).start())

    if_owner(reduce)

    def finish_y(source):
        y_copy(source, source).wait_recv()
        w_copy(source, source).wait_recv()

    each_other(finish_y)

    groups = []
    for d in range(0, n, 2):
        groups.append(w_in[d].astype(f32) + pltpu.roll(w_in[d + 1].astype(f32), slots, 1))
    weight = jnp.concatenate(groups, axis=1) * conf_scale
    ys = y_in[...].reshape(n * slots, y_in.shape[2])

    def sparse(v3, target):
        inner = add_pieces(nt(v3, ys))
        coeffs = weight * (1.0 - inner) if target else weight * inner
        return add_pieces(jnp.dot(pieces(coeffs), ys, preferred_element_type=f32))

    factors = start[...]
    v3 = pieces(factors)
    residual = sparse(v3, True)

    each_owner(lambda source: s_copy(source, source).wait_recv())
    per_rows = tri_sum[...].reshape(3 * half, half)
    cross = per_rows[half : 2 * half]
    shared = jnp.concatenate(
        [
            jnp.concatenate([per_rows[:half], cross], axis=1),
            jnp.concatenate([cross.T, per_rows[2 * half :]], axis=1),
        ],
        axis=0,
    )
    shared3 = pieces(shared)

    def dense(v, v3):
        wide = add_pieces(nt(v3, shared3))
        rank = v.shape[1]
        return wide[:, :rank] + wide[:, rank : 2 * rank] + wide[:, 2 * rank :] + damping * v

    residual = residual - dense(factors, v3)
    direction = residual
    norm_now = jnp.sum(residual * residual, axis=1, keepdims=True)
    for sweep in range(ITERS):
        v3 = pieces(direction)
        image = sparse(v3, False) + dense(direction, v3)
        step = norm_now / (jnp.sum(direction * image, axis=1, keepdims=True) + epsilon)
        factors = factors + step * direction
        if sweep + 1 < ITERS:
            residual = residual - step * image
            norm_next = jnp.sum(residual * residual, axis=1, keepdims=True)
            direction = residual + (norm_next / (norm_now + epsilon)) * direction
            norm_now = norm_next
    out[...] = factors

    def sent(to):
        y_copy(to, me).wait_send()
        w_copy(to, me).wait_send()

    each_other(sent)
    each_owner(lambda to: g_copy(to, me).wait_send())
    if_owner(lambda: each_other(lambda to: s_copy(to, me).wait_send()))


def shards(build_factors, nz_build, nz_test, nz_count, start_factors):
    tests, rank = start_factors.shape
    bld_rows = build_factors.shape[0]
    nz_rows = nz_build.shape[0]
    n = lax.axis_size("builds")
    conf_scale = n * bld_rows * tests / (8.0 * nz_rows)
    damping = 0.4 * conf_scale
    ids = nz_test[:, 0]
    number = jnp.arange(nz_rows, dtype=jnp.int32)
    earlier = (ids[:, None] == ids[None, :]) & (number[:, None] < number[None, :])
    slot = (ids * MOST + jnp.sum(earlier, axis=0, dtype=jnp.int32))[None, :]
    count = jnp.broadcast_to(nz_count.astype(bf16)[None, :], (tests, nz_rows))
    picked = build_factors[nz_build]

    slots = tests * MOST
    half = rank // 2
    part = 8
    tiles = 3 * half // part
    owners = max(k for k in range(1, min(n, tiles) + 1) if tiles % k == 0)
    share = tiles // owners
    chunk = 2048
    chunks = bld_rows // chunk
    vmem = pl.BlockSpec(memory_space=pltpu.VMEM)
    dma = pltpu.SemaphoreType.DMA
    return pl.pallas_call(
        functools.partial(kernel, n, owners, conf_scale, damping),
        out_shape=jax.ShapeDtypeStruct((tests, rank), f32),
        in_specs=[pl.BlockSpec(memory_space=pl.ANY)] + [vmem] * 4,
        out_specs=vmem,
        scratch_shapes=[
            pltpu.VMEM((chunks, chunk, rank), bf16),
            pltpu.VMEM((rank, rank), f32),
            pltpu.VMEM((tiles, part, half), f32),
            pltpu.VMEM((n, share, part, half), f32),
            pltpu.VMEM((tiles, part, half), f32),
            pltpu.VMEM((n, slots, rank), bf16),
            pltpu.VMEM((n, slots, rank), bf16),
            pltpu.VMEM((n, tests, 128), bf16),
            pltpu.VMEM((n, tests, 128), bf16),
            dma((chunks,)),
        ]
        + [dma((n,))] * 8,
        compiler_params=pltpu.CompilerParams(
            collective_id=0, has_side_effects=True, vmem_limit_bytes=48 * 1024 * 1024
        ),
    )(build_factors, picked, slot, count, start_factors)


def solution(mesh):
    return jax.shard_map(
        shards,
        mesh=mesh,
        in_specs=(
            P("builds", None),
            P(("groups", "builds")),
            P(("groups", "builds"), None),
            P(("groups", "builds")),
            P(("groups", "builds"), None),
        ),
        out_specs=P(("groups", "builds"), None),
        check_vma=False,
    )
```

```python
import functools

import jax
import jax.numpy as jnp
from jax import lax
from jax.experimental import pallas as pl
from jax.experimental.pallas import tpu as pltpu
from jax.sharding import PartitionSpec as P

ITERS = 3
MOST = 4
epsilon = 1e-06
f32 = jnp.float32
bf16 = jnp.bfloat16


def pieces(v):
    high = v.astype(bf16)
    rest = v - high.astype(f32)
    mid = rest.astype(bf16)
    low = (rest - mid.astype(f32)).astype(bf16)
    return jnp.concatenate([high, mid, low], axis=0)


def add_pieces(v):
    rows = v.shape[0] // 3
    return v[:rows] + v[rows : 2 * rows] + v[2 * rows :]


def nt(a, b):
    return lax.dot_general(a, b, (((1,), (1,)), ((), ())), preferred_element_type=f32)


def tn(a, b):
    return lax.dot_general(a, b, (((0,), (0,)), ((), ())), preferred_element_type=f32)


def kernel(
    n, owners, conf_scale, damping,
    nz_at, x_hbm, nz_row, test_row, count_row, start, out,
    x_buf, picked, slot, select, gram, tri, tri_in, tri_sum, y_out, y_in, w_out, w_in,
    x_sem, y_send, y_recv, w_send, w_recv, g_send, g_recv, s_send, s_recv,
):
    me = lax.axis_index("builds")
    chunks = x_sem.shape[0]
    lumps, lump, rank = x_buf.shape
    chunk = lumps // chunks
    nz = slot.shape[1]
    tests = start.shape[0]
    slots = tests * MOST
    width = w_out.shape[2]
    part = tri.shape[1]
    half = tri.shape[2]

    def load(c):
        return pltpu.make_async_copy(
            x_hbm.at[pl.ds(c * chunk, chunk)], x_buf.at[pl.ds(c * chunk, chunk)], x_sem.at[c]
        )

    @pl.loop(0, chunks)
    def _(c):
        load(c).start()

    barrier = pltpu.get_barrier_semaphore()

    @pl.loop(1, n)
    def _(j):
        pl.semaphore_signal(
            barrier, inc=1, device_id={"builds": lax.rem(me + j, n)}, device_id_type=pl.DeviceIdType.MESH
        )

    tests_at = jnp.broadcast_to(test_row[...].astype(f32), (128, nz)).T

    @pl.loop(0, nz // 128)
    def _(c):
        lanes = pl.ds(pl.multiple_of(c * 128, 128), 128)
        ids = test_row[:, lanes]
        first = lax.broadcasted_iota(jnp.int32, (nz, 128), 0)
        second = lax.broadcasted_iota(jnp.int32, (nz, 128), 1) + c * 128
        same = (tests_at == ids.astype(f32)) & (first < second)
        earlier = jnp.sum(same.astype(f32), axis=0, keepdims=True)
        slot[:, lanes] = ids * MOST + earlier.astype(jnp.int32)

    number = lax.broadcasted_iota(jnp.int32, (1, nz), 1)
    place = (number % lump) * lump + nz_row[...] % lump
    column = lax.broadcasted_iota(jnp.int32, (lump * lump, nz), 0)
    select[...] = (column == place).astype(f32).T.astype(bf16)
    count = jnp.broadcast_to(count_row[...].astype(f32), (tests, nz)).astype(bf16)

    def remote(src, dst, send, recv, to):
        return pltpu.make_async_remote_copy(
            src_ref=src, dst_ref=dst, send_sem=send, recv_sem=recv,
            device_id={"builds": to}, device_id_type=pl.DeviceIdType.MESH,
        )

    def y_copy(to, source):
        return remote(y_out.at[to], y_in.at[source], y_send.at[to], y_recv.at[source], to)

    def w_copy(to, source):
        return remote(w_out.at[to], w_in.at[source], w_send.at[to], w_recv.at[source], to)

    def block_of(owner):
        local = slot[...] - owner * slots
        local = jnp.where((local >= 0) & (local < slots), local, -1)
        row = lax.broadcasted_iota(jnp.int32, (width, local.shape[1]), 0)
        place = (row == local).astype(f32).astype(bf16)
        rows = jnp.dot(place[:slots], picked[...], preferred_element_type=f32).astype(bf16)
        counts = nt(count, place)
        test = lax.broadcasted_iota(jnp.int32, counts.shape, 0)
        lane = lax.broadcasted_iota(jnp.int32, counts.shape, 1)
        return rows, jnp.where(lane // MOST == test, counts, 0.0).astype(bf16)

    gram[...] = jnp.zeros_like(gram)

    @pl.loop(0, chunks)
    def _(c):
        load(c).wait()
        x = x_buf[pl.ds(c * chunk, chunk)].reshape(chunk * lump, rank)
        gram[...] += tn(x, x)

    per = half // part
    for i in range(per):
        tri[i] = gram[i * part : (i + 1) * part, :half]
        tri[per + i] = gram[i * part : (i + 1) * part, half:]
        tri[2 * per + i] = gram[half + i * part : half + (i + 1) * part, half:]

    share = tri.shape[0] // owners

    def g_copy(to, source):
        return remote(
            tri.at[pl.ds(to * share, share)], tri_in.at[source], g_send.at[to], g_recv.at[source], to
        )

    def s_copy(to, source):
        tiles = pl.ds(source * share, share)
        return remote(tri_sum.at[tiles], tri_sum.at[tiles], s_send.at[to], s_recv.at[source], to)

    def each_owner(body):
        @pl.loop(1, n)
        def _(j):
            other = lax.rem(me + j, n)
            if owners == n:
                body(other)
            else:
                pl.when(other < owners)(lambda: body(other))

    def each_other(body):
        @pl.loop(1, n)
        def _(j):
            body(lax.rem(me + j, n))

    def if_owner(body):
        if owners == n:
            body()
        else:
            pl.when(me < owners)(body)

    pl.semaphore_wait(barrier, n - 1)
    each_owner(lambda to: g_copy(to, me).start())

    @pl.loop(0, nz // lump)
    def _(b):
        near = jnp.concatenate([x_buf[nz_at[b * lump + i] // lump] for i in range(lump)], axis=0)
        rows = pl.ds(pl.multiple_of(b * lump, lump), lump)
        picked[rows, :] = jnp.dot(select[rows, :], near, preferred_element_type=f32).astype(bf16)

    rows, counts = block_of(me)
    y_in[me] = rows
    w_in[me] = counts

    @pl.loop(1, n)
    def _(j):
        to = lax.rem(me + j, n)
        rows, counts = block_of(to)
        y_out[to] = rows
        w_out[to] = counts
        y_copy(to, me).start()
        w_copy(to, me).start()


    def reduce():
        tri_in[me] = tri[pl.ds(me * share, share)]
        each_other(lambda source: g_copy(me, source).wait_recv())
        tri_sum[pl.ds(me * share, share)] = jnp.sum(tri_in[...], axis=0)
        each_other(lambda to: s_copy(to, me).start())

    if_owner(reduce)

    def finish_y(source):
        y_copy(source, source).wait_recv()
        w_copy(source, source).wait_recv()

    each_other(finish_y)

    groups = []
    for d in range(0, n, 2):
        groups.append(w_in[d].astype(f32) + pltpu.roll(w_in[d + 1].astype(f32), slots, 1))
    weight = jnp.concatenate(groups, axis=1) * conf_scale
    ys = y_in[...].reshape(n * slots, y_in.shape[2])

    def sparse(v3, target):
        inner = add_pieces(nt(v3, ys))
        coeffs = weight * (1.0 - inner) if target else weight * inner
        return add_pieces(jnp.dot(pieces(coeffs), ys, preferred_element_type=f32))

    factors = start[...]
    v3 = pieces(factors)
    residual = sparse(v3, True)

    each_owner(lambda source: s_copy(source, source).wait_recv())
    per_rows = tri_sum[...].reshape(3 * half, half)
    cross = per_rows[half : 2 * half]
    shared = jnp.concatenate(
        [
            jnp.concatenate([per_rows[:half], cross], axis=1),
            jnp.concatenate([cross.T, per_rows[2 * half :]], axis=1),
        ],
        axis=0,
    )
    shared3 = pieces(shared)

    def dense(v, v3):
        wide = add_pieces(nt(v3, shared3))
        rank = v.shape[1]
        return wide[:, :rank] + wide[:, rank : 2 * rank] + wide[:, 2 * rank :] + damping * v

    residual = residual - dense(factors, v3)
    direction = residual
    norm_now = jnp.sum(residual * residual, axis=1, keepdims=True)
    for sweep in range(ITERS):
        v3 = pieces(direction)
        image = sparse(v3, False) + dense(direction, v3)
        step = norm_now / (jnp.sum(direction * image, axis=1, keepdims=True) + epsilon)
        factors = factors + step * direction
        if sweep + 1 < ITERS:
            residual = residual - step * image
            norm_next = jnp.sum(residual * residual, axis=1, keepdims=True)
            direction = residual + (norm_next / (norm_now + epsilon)) * direction
            norm_now = norm_next
    out[...] = factors

    def sent(to):
        y_copy(to, me).wait_send()
        w_copy(to, me).wait_send()

    each_other(sent)
    each_owner(lambda to: g_copy(to, me).wait_send())
    if_owner(lambda: each_other(lambda to: s_copy(to, me).wait_send()))


def shards(build_factors, nz_build, nz_test, nz_count, start_factors):
    tests, rank = start_factors.shape
    bld_rows = build_factors.shape[0]
    nz_rows = nz_build.shape[0]
    n = lax.axis_size("builds")
    conf_scale = n * bld_rows * tests / (8.0 * nz_rows)
    damping = 0.4 * conf_scale
    slots = tests * MOST
    half = rank // 2
    part = 8
    tiles = 3 * half // part
    owners = max(k for k in range(1, min(n, tiles) + 1) if tiles % k == 0)
    share = tiles // owners
    lump = 16
    chunks = bld_rows // 2048
    vmem = pl.BlockSpec(memory_space=pltpu.VMEM)
    dma = pltpu.SemaphoreType.DMA
    return pl.pallas_call(
        functools.partial(kernel, n, owners, conf_scale, damping),
        out_shape=jax.ShapeDtypeStruct((tests, rank), f32),
        in_specs=[pl.BlockSpec(memory_space=pltpu.SMEM), pl.BlockSpec(memory_space=pl.ANY)] + [vmem] * 4,
        out_specs=vmem,
        scratch_shapes=[
            pltpu.VMEM((bld_rows // lump, lump, rank), bf16),
            pltpu.VMEM((nz_rows, rank), bf16),
            pltpu.VMEM((1, nz_rows), jnp.int32),
            pltpu.VMEM((nz_rows, lump * lump), bf16),
            pltpu.VMEM((rank, rank), f32),
            pltpu.VMEM((tiles, part, half), f32),
            pltpu.VMEM((n, share, part, half), f32),
            pltpu.VMEM((tiles, part, half), f32),
            pltpu.VMEM((n, slots, rank), bf16),
            pltpu.VMEM((n, slots, rank), bf16),
            pltpu.VMEM((n, tests, 128), bf16),
            pltpu.VMEM((n, tests, 128), bf16),
            dma((chunks,)),
        ]
        + [dma((n,))] * 8,
        compiler_params=pltpu.CompilerParams(
            collective_id=0, has_side_effects=True, vmem_limit_bytes=48 * 1024 * 1024
        ),
    )(
        nz_build,
        build_factors.reshape(bld_rows // lump, lump, rank),
        nz_build[None, :],
        nz_test.reshape(1, nz_rows),
        nz_count[None, :],
        start_factors,
    )


def solution(mesh):
    return jax.shard_map(
        shards,
        mesh=mesh,
        in_specs=(
            P("builds", None),
            P(("groups", "builds")),
            P(("groups", "builds"), None),
            P(("groups", "builds")),
            P(("groups", "builds"), None),
        ),
        out_specs=P(("groups", "builds"), None),
        check_vma=False,
    )
```

```python
import functools

import jax
import jax.numpy as jnp
from jax import lax
from jax.experimental import pallas as pl
from jax.experimental.pallas import tpu as pltpu
from jax.sharding import PartitionSpec as P

ITERS = 3
MOST = 4
PLANE = 4
epsilon = 1e-06
f32 = jnp.float32
bf16 = jnp.bfloat16


def pieces(v):
    high = v.astype(bf16)
    rest = v - high.astype(f32)
    mid = rest.astype(bf16)
    low = (rest - mid.astype(f32)).astype(bf16)
    return jnp.concatenate([high, mid, low], axis=0)


def add_pieces(v):
    rows = v.shape[0] // 3
    return v[:rows] + v[rows : 2 * rows] + v[2 * rows :]


def nt(a, b):
    return lax.dot_general(a, b, (((1,), (1,)), ((), ())), preferred_element_type=f32)


def tn(a, b):
    return lax.dot_general(a, b, (((0,), (0,)), ((), ())), preferred_element_type=f32)


def kernel(
    n, owners, conf_scale, damping,
    nz_hbm, test_hbm, count_hbm, start_hbm, x_hbm, out,
    nz_row, test_row, count_row, start, x_buf, slot, packed, counts_at, at_vmem, at, select, gram,
    tri, plane_in, plane_sum, line_in, tri_sum, y_out, y_in, w_out, w_in,
    x_sem, in_sem, y_send, y_recv, w_send, w_recv,
    a_send, a_recv, b_send, b_recv, c_send, c_recv, d_send, d_recv,
):
    me = lax.axis_index("builds")
    chunks = x_sem.shape[0]
    lumps, lump, rank = x_buf.shape
    chunk = lumps // chunks
    nz = slot.shape[1]
    tests = start.shape[0]
    slots = tests * MOST
    part = tri.shape[1]
    half = tri.shape[2]
    tiles = tri.shape[0]
    line = n // PLANE
    z, p = me // PLANE, lax.rem(me, PLANE)

    small = [
        pltpu.make_async_copy(src, dst, in_sem.at[i])
        for i, (src, dst) in enumerate(
            [(nz_hbm, nz_row), (test_hbm, test_row), (count_hbm, count_row), (start_hbm, start)]
        )
    ]
    for copy in small:
        copy.start()

    def load(c):
        return pltpu.make_async_copy(
            x_hbm.at[pl.ds(c * chunk, chunk)], x_buf.at[pl.ds(c * chunk, chunk)], x_sem.at[c]
        )

    @pl.loop(0, chunks)
    def _(c):
        load(c).start()

    barrier = pltpu.get_barrier_semaphore()

    @pl.loop(1, n)
    def _(j):
        pl.semaphore_signal(
            barrier, inc=1, device_id={"builds": lax.rem(me + j, n)}, device_id_type=pl.DeviceIdType.MESH
        )

    for copy in small:
        copy.wait()

    tests_at = jnp.broadcast_to(test_row[...], (128, nz)).T

    @pl.loop(0, nz // 128)
    def _(c):
        lanes = pl.ds(pl.multiple_of(c * 128, 128), 128)
        ids = test_row[:, lanes]
        first = lax.broadcasted_iota(jnp.int32, (nz, 128), 0)
        second = lax.broadcasted_iota(jnp.int32, (nz, 128), 1) + c * 128
        same = (tests_at == ids) & (first < second)
        earlier = jnp.sum(same.astype(jnp.int32), axis=0, keepdims=True)
        slot[:, lanes] = ids * MOST + earlier

    slot_at = jnp.broadcast_to(slot[...], (128, nz)).T
    packed[...] = jnp.broadcast_to(nz_row[...] * 16 + count_row[...], (128, nz)).T

    @pl.loop(0, n * slots // 128)
    def _(c):
        lane = lax.broadcasted_iota(jnp.int32, (1, 128), 1)
        wanted = lane + c * 128
        held = jnp.sum(jnp.where(slot_at == wanted, packed[...], 0), axis=0, keepdims=True)
        row, amount = held // 16, held % 16
        at_vmem[pl.ds(c, 1), :] = jnp.clip(row // lump, 0, lumps - 1)
        counts_at[pl.ds(c, 1), :] = amount.astype(f32)
        place = jnp.where(amount > 0, (lane % lump) * lump + row % lump, -1)
        place = jnp.broadcast_to(place.astype(f32), (128, 128)).T
        column = lax.broadcasted_iota(jnp.int32, (128, 128), 1).astype(f32)
        both = [(place == column + h * 128.0).astype(f32) for h in range(lump * lump // 128)]
        select[pl.ds(pl.multiple_of(c * 128, 128), 128), :] = jnp.concatenate(both, axis=1).astype(bf16)

    to_scalars = pltpu.make_async_copy(at_vmem, at, in_sem.at[0])
    to_scalars.start()

    def remote(src, dst, send, recv, to):
        return pltpu.make_async_remote_copy(
            src_ref=src, dst_ref=dst, send_sem=send, recv_sem=recv,
            device_id={"builds": to}, device_id_type=pl.DeviceIdType.MESH,
        )

    def y_copy(to, source):
        return remote(y_out.at[to], y_in.at[source], y_send.at[to], y_recv.at[source], to)

    def w_copy(to, source):
        return remote(w_out.at[to], w_in.at[source], w_send.at[to], w_recv.at[source], to)

    pair = 128 // slots

    def block_of(owner):
        line_at, lane_at = owner // pair, lax.rem(owner, pair) * slots
        rows = []
        for b in range(slots // lump):
            near = jnp.concatenate(
                [x_buf[at[line_at, lane_at + b * lump + i]] for i in range(lump)], axis=0
            )
            chosen = select[pl.ds(pl.multiple_of(owner * slots + b * lump, lump), lump), :]
            rows.append(jnp.dot(chosen, near, preferred_element_type=f32).astype(bf16))
        counts = jnp.broadcast_to(counts_at[pl.ds(line_at, 1), :], (tests, 128))
        counts = pltpu.roll(counts, lax.rem(128 - lane_at, 128), 1)
        test = lax.broadcasted_iota(jnp.int32, counts.shape, 0)
        lane = lax.broadcasted_iota(jnp.int32, counts.shape, 1)
        return jnp.concatenate(rows, axis=0), jnp.where(lane // MOST == test, counts, 0.0).astype(bf16)

    gram[...] = jnp.zeros_like(gram)

    @pl.loop(0, chunks)
    def _(c):
        load(c).wait()
        x = x_buf[pl.ds(c * chunk, chunk)].reshape(chunk * lump, rank)
        gram[...] += tn(x, x)

    per = half // part
    for i in range(per):
        tri[i] = gram[i * part : (i + 1) * part, :half]
        tri[per + i] = gram[i * part : (i + 1) * part, half:]
        tri[2 * per + i] = gram[half + i * part : half + (i + 1) * part, half:]

    quarter = tiles // PLANE
    share = quarter // owners

    def in_plane(body):
        for k in range(1, PLANE):
            body(lax.rem(p + k, PLANE))

    def in_line(body, only_owners=False):
        @pl.loop(1, line)
        def _(k):
            other = lax.rem(z + k, line)
            if only_owners and owners < line:
                pl.when(other < owners)(lambda: body(other))
            else:
                body(other)

    def if_owner(body):
        if owners == line:
            body()
        else:
            pl.when(z < owners)(body)

    def a_copy(to, source):
        return remote(
            tri.at[pl.ds(to * quarter, quarter)], plane_in.at[source],
            a_send.at[to], a_recv.at[source], z * PLANE + to,
        )

    def b_copy(to, source):
        return remote(
            plane_sum.at[pl.ds(to * share, share)], line_in.at[source],
            b_send.at[to], b_recv.at[source], to * PLANE + p,
        )

    def c_copy(to, source):
        there = pl.ds(p * quarter + source * share, share)
        return remote(tri_sum.at[there], tri_sum.at[there], c_send.at[to], c_recv.at[source], to * PLANE + p)

    def d_copy(to, source):
        there = pl.ds(source * quarter, quarter)
        return remote(tri_sum.at[there], tri_sum.at[there], d_send.at[to], d_recv.at[source], z * PLANE + to)

    def gather(first, last):
        @pl.loop(first, last)
        def _(u):
            turn = u // PLANE
            away = line // 2 + ((turn + 1) // 2) * (1 - 2 * lax.rem(turn + 1, 2))
            to = lax.rem(z + away, line) * PLANE + lax.rem(p + u + 1, PLANE)
            rows, counts = block_of(to)
            y_out[to] = rows
            w_out[to] = counts
            y_copy(to, me).start()
            w_copy(to, me).start()

    pl.semaphore_wait(barrier, n - 1)
    in_plane(lambda to: a_copy(to, p).start())
    to_scalars.wait()
    gather(0, n * 3 // 16)

    plane_in[p] = tri[pl.ds(p * quarter, quarter)]
    in_plane(lambda source: a_copy(p, source).wait_recv())
    plane_sum[...] = jnp.sum(plane_in[...], axis=0)
    in_line(lambda to: b_copy(to, z).start(), True)
    gather(n * 3 // 16, n * 6 // 16)

    def reduce():
        line_in[z] = plane_sum[pl.ds(z * share, share)]
        in_line(lambda source: b_copy(z, source).wait_recv())
        tri_sum[pl.ds(p * quarter + z * share, share)] = jnp.sum(line_in[...], axis=0)
        in_line(lambda to: c_copy(to, z).start())

    if_owner(reduce)
    gather(n * 6 // 16, n * 10 // 16)
    in_line(lambda source: c_copy(z, source).wait_recv(), True)
    in_plane(lambda to: d_copy(to, p).start())
    gather(n * 10 // 16, n - 1)
    rows, counts = block_of(me)
    y_in[me] = rows
    w_in[me] = counts

    in_plane(lambda source: d_copy(p, source).wait_recv())
    full = tri_sum[...].reshape(3 * half, half)
    cross = full[half : 2 * half]
    shared = jnp.concatenate(
        [
            jnp.concatenate([full[:half], cross], axis=1),
            jnp.concatenate([cross.T, full[2 * half :]], axis=1),
        ],
        axis=0,
    )
    shared3 = pieces(shared)

    def dense(v, v3):
        wide = add_pieces(nt(v3, shared3))
        return wide[:, :rank] + wide[:, rank : 2 * rank] + wide[:, 2 * rank :] + damping * v

    factors = start[...]
    v3 = pieces(factors)
    residual = -dense(factors, v3)

    def each_other(body):
        @pl.loop(1, n)
        def _(j):
            body(lax.rem(me + j, n))

    def finish_y(source):
        y_copy(me, source).wait_recv()
        w_copy(me, source).wait_recv()

    each_other(finish_y)

    groups = []
    for d in range(0, n, 2):
        groups.append(w_in[d].astype(f32) + pltpu.roll(w_in[d + 1].astype(f32), slots, 1))
    weight = jnp.concatenate(groups, axis=1) * conf_scale
    ys = y_in[...].reshape(n * slots, y_in.shape[2])

    def sparse(v3, target):
        inner = add_pieces(nt(v3, ys))
        coeffs = weight * (1.0 - inner) if target else weight * inner
        return add_pieces(jnp.dot(pieces(coeffs), ys, preferred_element_type=f32))

    residual = sparse(v3, True) + residual
    direction = residual
    norm_now = jnp.sum(residual * residual, axis=1, keepdims=True)
    for sweep in range(ITERS):
        v3 = pieces(direction)
        image = sparse(v3, False) + dense(direction, v3)
        step = norm_now / (jnp.sum(direction * image, axis=1, keepdims=True) + epsilon)
        factors = factors + step * direction
        if sweep + 1 < ITERS:
            residual = residual - step * image
            norm_next = jnp.sum(residual * residual, axis=1, keepdims=True)
            direction = residual + (norm_next / (norm_now + epsilon)) * direction
            norm_now = norm_next
    out[...] = factors

    def sent(to):
        y_copy(to, me).wait_send()
        w_copy(to, me).wait_send()

    each_other(sent)
    in_plane(lambda to: a_copy(to, p).wait_send())
    in_line(lambda to: b_copy(to, z).wait_send(), True)
    if_owner(lambda: in_line(lambda to: c_copy(to, z).wait_send()))
    in_plane(lambda to: d_copy(to, p).wait_send())


def shards(build_factors, nz_build, nz_test, nz_count, start_factors):
    tests, rank = start_factors.shape
    bld_rows = build_factors.shape[0]
    nz_rows = nz_build.shape[0]
    n = lax.axis_size("builds")
    conf_scale = n * bld_rows * tests / (8.0 * nz_rows)
    damping = 0.4 * conf_scale
    slots = tests * MOST
    half = rank // 2
    part = 8
    tiles = 3 * half // part
    line = n // PLANE
    quarter = tiles // PLANE
    owners = max(k for k in range(1, min(line, quarter) + 1) if quarter % k == 0)
    share = quarter // owners
    lump = 16
    chunks = bld_rows // 2048
    lines = n * slots // 128
    dma = pltpu.SemaphoreType.DMA
    return pl.pallas_call(
        functools.partial(kernel, n, owners, conf_scale, damping),
        out_shape=jax.ShapeDtypeStruct((tests, rank), f32),
        in_specs=[pl.BlockSpec(memory_space=pltpu.HBM)] * 5,
        out_specs=pl.BlockSpec(memory_space=pltpu.VMEM),
        scratch_shapes=[
            pltpu.VMEM((1, nz_rows), jnp.int32),
            pltpu.VMEM((1, nz_rows), jnp.int32),
            pltpu.VMEM((1, nz_rows), jnp.int32),
            pltpu.VMEM((tests, rank), f32),
            pltpu.VMEM((bld_rows // lump, lump, rank), bf16),
            pltpu.VMEM((1, nz_rows), jnp.int32),
            pltpu.VMEM((nz_rows, 128), jnp.int32),
            pltpu.VMEM((lines, 128), f32),
            pltpu.VMEM((lines, 128), jnp.int32),
            pltpu.SMEM((lines, 128), jnp.int32),
            pltpu.VMEM((n * slots, lump * lump), bf16),
            pltpu.VMEM((rank, rank), f32),
            pltpu.VMEM((tiles, part, half), f32),
            pltpu.VMEM((PLANE, quarter, part, half), f32),
            pltpu.VMEM((quarter, part, half), f32),
            pltpu.VMEM((line, share, part, half), f32),
            pltpu.VMEM((tiles, part, half), f32),
            pltpu.VMEM((n, slots, rank), bf16),
            pltpu.VMEM((n, slots, rank), bf16),
            pltpu.VMEM((n, tests, 128), bf16),
            pltpu.VMEM((n, tests, 128), bf16),
            dma((chunks,)),
            dma((4,)),
        ]
        + [dma((n,))] * 4
        + [dma((PLANE,))] * 2
        + [dma((line,))] * 4
        + [dma((PLANE,))] * 2,
        compiler_params=pltpu.CompilerParams(
            collective_id=0, has_side_effects=True, vmem_limit_bytes=64 * 1024 * 1024
        ),
    )(
        nz_build[None, :],
        nz_test.reshape(1, nz_rows),
        nz_count[None, :],
        start_factors,
        build_factors.reshape(bld_rows // lump, lump, rank),
    )


def solution(mesh):
    return jax.shard_map(
        shards,
        mesh=mesh,
        in_specs=(
            P("builds", None),
            P(("groups", "builds")),
            P(("groups", "builds"), None),
            P(("groups", "builds")),
            P(("groups", "builds"), None),
        ),
        out_specs=P(("groups", "builds"), None),
        check_vma=False,
    )
```

```python
import functools

import jax
import jax.numpy as jnp
from jax import lax
from jax.experimental import pallas as pl
from jax.experimental.pallas import tpu as pltpu
from jax.sharding import PartitionSpec as P

ITERS = 3
MOST = 4
PLANE = 4
epsilon = 1e-06
f32 = jnp.float32
bf16 = jnp.bfloat16


def pieces(v):
    high = v.astype(bf16)
    rest = v - high.astype(f32)
    mid = rest.astype(bf16)
    low = (rest - mid.astype(f32)).astype(bf16)
    return jnp.concatenate([high, mid, low], axis=0)


def add_pieces(v):
    rows = v.shape[0] // 3
    return v[:rows] + v[rows : 2 * rows] + v[2 * rows :]


def nt(a, b):
    return lax.dot_general(a, b, (((1,), (1,)), ((), ())), preferred_element_type=f32)


def tn(a, b):
    return lax.dot_general(a, b, (((0,), (0,)), ((), ())), preferred_element_type=f32)


def kernel(
    n, owners, conf_scale, damping,
    nz_hbm, test_hbm, count_hbm, start_hbm, x_hbm, out,
    nz_row, test_row, count_row, start, x_buf, slot, packed, counts_at, at_vmem, at, select, gram,
    tri, plane_in, plane_sum, line_in, tri_sum, y_out, y_in, w_out, w_in,
    x_sem, in_sem, y_send, y_recv, w_send, w_recv,
    a_send, a_recv, b_send, b_recv, c_send, c_recv, d_send, d_recv,
):
    me = lax.axis_index("builds")
    chunks = x_sem.shape[0]
    lumps, lump, rank = x_buf.shape
    chunk = lumps // chunks
    nz = slot.shape[1]
    tests = start.shape[0]
    slots = tests * MOST
    part = tri.shape[1]
    half = tri.shape[2]
    tiles = tri.shape[0]
    line = n // PLANE
    z, p = me // PLANE, lax.rem(me, PLANE)

    small = [
        pltpu.make_async_copy(src, dst, in_sem.at[i])
        for i, (src, dst) in enumerate(
            [(nz_hbm, nz_row), (test_hbm, test_row), (count_hbm, count_row), (start_hbm, start)]
        )
    ]
    for copy in small:
        copy.start()

    def load(c):
        return pltpu.make_async_copy(
            x_hbm.at[pl.ds(c * chunk, chunk)], x_buf.at[pl.ds(c * chunk, chunk)], x_sem.at[c]
        )

    @pl.loop(0, chunks)
    def _(c):
        load(c).start()

    barrier = pltpu.get_barrier_semaphore()

    @pl.loop(1, n)
    def _(j):
        pl.semaphore_signal(
            barrier, inc=1, device_id={"builds": lax.rem(me + j, n)}, device_id_type=pl.DeviceIdType.MESH
        )

    for copy in small:
        copy.wait()

    tests_at = jnp.broadcast_to(test_row[...], (128, nz)).T

    @pl.loop(0, nz // 128)
    def _(c):
        lanes = pl.ds(pl.multiple_of(c * 128, 128), 128)
        ids = test_row[:, lanes]
        first = lax.broadcasted_iota(jnp.int32, (nz, 128), 0)
        second = lax.broadcasted_iota(jnp.int32, (nz, 128), 1) + c * 128
        same = (tests_at == ids) & (first < second)
        earlier = jnp.sum(same.astype(jnp.int32), axis=0, keepdims=True)
        slot[:, lanes] = ids * MOST + earlier

    slot_at = jnp.broadcast_to(slot[...], (128, nz)).T
    packed[...] = jnp.broadcast_to(nz_row[...] * 16 + count_row[...], (128, nz)).T

    @pl.loop(0, n * slots // 128)
    def _(c):
        lane = lax.broadcasted_iota(jnp.int32, (1, 128), 1)
        wanted = lane + c * 128
        held = jnp.sum(jnp.where(slot_at == wanted, packed[...], 0), axis=0, keepdims=True)
        row, amount = held // 16, held % 16
        at_vmem[pl.ds(c, 1), :] = jnp.clip(row // lump, 0, lumps - 1)
        counts_at[pl.ds(c, 1), :] = amount.astype(f32)
        place = jnp.where(amount > 0, (lane % lump) * lump + row % lump, -1)
        place = jnp.broadcast_to(place.astype(f32), (128, 128)).T
        column = lax.broadcasted_iota(jnp.int32, (128, 128), 1).astype(f32)
        both = [(place == column + h * 128.0).astype(f32) for h in range(lump * lump // 128)]
        select[pl.ds(pl.multiple_of(c * 128, 128), 128), :] = jnp.concatenate(both, axis=1).astype(bf16)

    to_scalars = pltpu.make_async_copy(at_vmem, at, in_sem.at[0])
    to_scalars.start()

    def remote(src, dst, send, recv, to):
        return pltpu.make_async_remote_copy(
            src_ref=src, dst_ref=dst, send_sem=send, recv_sem=recv,
            device_id={"builds": to}, device_id_type=pl.DeviceIdType.MESH,
        )

    def y_copy(to, source):
        return remote(y_out.at[to], y_in.at[source], y_send.at[to], y_recv.at[source], to)

    def w_copy(to, source):
        return remote(w_out.at[to], w_in.at[source], w_send.at[to], w_recv.at[source], to)

    pair = 128 // slots

    def block_of(owner):
        line_at, lane_at = owner // pair, lax.rem(owner, pair) * slots
        rows = []
        for b in range(slots // lump):
            near = jnp.concatenate(
                [x_buf[at[line_at, lane_at + b * lump + i]] for i in range(lump)], axis=0
            )
            chosen = select[pl.ds(pl.multiple_of(owner * slots + b * lump, lump), lump), :]
            rows.append(jnp.dot(chosen, near, preferred_element_type=f32).astype(bf16))
        counts = jnp.broadcast_to(counts_at[pl.ds(line_at, 1), :], (tests, 128))
        counts = pltpu.roll(counts, lax.rem(128 - lane_at, 128), 1)
        test = lax.broadcasted_iota(jnp.int32, counts.shape, 0)
        lane = lax.broadcasted_iota(jnp.int32, counts.shape, 1)
        return jnp.concatenate(rows, axis=0), jnp.where(lane // MOST == test, counts, 0.0).astype(bf16)

    gram[...] = jnp.zeros_like(gram)

    def add_gram(c):
        x = x_buf[pl.ds(c * chunk, chunk)].reshape(chunk * lump, rank)
        gram[...] += tn(x, x)

    early = max(chunks * 5 // 12, chunks - (n - 1))
    late = chunks - early

    @pl.loop(0, early)
    def _(c):
        load(c).wait()
        add_gram(c)

    @pl.loop(early, chunks)
    def _(c):
        load(c).wait()

    quarter = tiles // PLANE
    share = quarter // owners

    def in_plane(body):
        for k in range(1, PLANE):
            body(lax.rem(p + k, PLANE))

    def in_line(body, only_owners=False):
        @pl.loop(1, line)
        def _(k):
            other = lax.rem(z + k, line)
            if only_owners and owners < line:
                pl.when(other < owners)(lambda: body(other))
            else:
                body(other)

    def if_owner(body):
        if owners == line:
            body()
        else:
            pl.when(z < owners)(body)

    def a_copy(to, source):
        return remote(
            tri.at[pl.ds(to * quarter, quarter)], plane_in.at[source],
            a_send.at[to], a_recv.at[source], z * PLANE + to,
        )

    def b_copy(to, source):
        return remote(
            plane_sum.at[pl.ds(to * share, share)], line_in.at[source],
            b_send.at[to], b_recv.at[source], to * PLANE + p,
        )

    def c_copy(to, source):
        there = pl.ds(p * quarter + source * share, share)
        return remote(tri_sum.at[there], tri_sum.at[there], c_send.at[to], c_recv.at[source], to * PLANE + p)

    def d_copy(to, source):
        there = pl.ds(source * quarter, quarter)
        return remote(tri_sum.at[there], tri_sum.at[there], d_send.at[to], d_recv.at[source], z * PLANE + to)

    def gather(first, last, with_gram=False):
        @pl.loop(first, last)
        def _(u):
            turn = u // PLANE
            away = line // 2 + ((turn + 1) // 2) * (1 - 2 * lax.rem(turn + 1, 2))
            to = lax.rem(z + away, line) * PLANE + lax.rem(p + u + 1, PLANE)
            rows, counts = block_of(to)
            y_out[to] = rows
            w_out[to] = counts
            y_copy(to, me).start()
            w_copy(to, me).start()
            if with_gram:
                add_gram(early + u)

    pl.semaphore_wait(barrier, n - 1)
    to_scalars.wait()
    gather(0, late, True)

    per = half // part
    for i in range(per):
        tri[i] = gram[i * part : (i + 1) * part, :half]
        tri[per + i] = gram[i * part : (i + 1) * part, half:]
        tri[2 * per + i] = gram[half + i * part : half + (i + 1) * part, half:]

    in_plane(lambda to: a_copy(to, p).start())
    cuts = [late + (n - 1 - late) * i // 4 for i in range(5)]
    gather(cuts[0], cuts[1])

    plane_in[p] = tri[pl.ds(p * quarter, quarter)]
    in_plane(lambda source: a_copy(p, source).wait_recv())
    plane_sum[...] = jnp.sum(plane_in[...], axis=0)
    in_line(lambda to: b_copy(to, z).start(), True)
    gather(cuts[1], cuts[2])

    def reduce():
        line_in[z] = plane_sum[pl.ds(z * share, share)]
        in_line(lambda source: b_copy(z, source).wait_recv())
        tri_sum[pl.ds(p * quarter + z * share, share)] = jnp.sum(line_in[...], axis=0)
        in_line(lambda to: c_copy(to, z).start())

    if_owner(reduce)
    gather(cuts[2], cuts[3])
    in_line(lambda source: c_copy(z, source).wait_recv(), True)
    in_plane(lambda to: d_copy(to, p).start())
    gather(cuts[3], cuts[4])
    rows, counts = block_of(me)
    y_in[me] = rows
    w_in[me] = counts

    in_plane(lambda source: d_copy(p, source).wait_recv())
    full = tri_sum[...].reshape(3 * half, half)
    cross = full[half : 2 * half]
    shared = jnp.concatenate(
        [
            jnp.concatenate([full[:half], cross], axis=1),
            jnp.concatenate([cross.T, full[2 * half :]], axis=1),
        ],
        axis=0,
    )
    shared3 = pieces(shared)

    def dense(v, v3):
        wide = add_pieces(nt(v3, shared3))
        return wide[:, :rank] + wide[:, rank : 2 * rank] + wide[:, 2 * rank :] + damping * v

    factors = start[...]
    v3 = pieces(factors)
    residual = -dense(factors, v3)

    def each_other(body):
        @pl.loop(1, n)
        def _(j):
            body(lax.rem(me + j, n))

    def finish_y(source):
        y_copy(me, source).wait_recv()
        w_copy(me, source).wait_recv()

    each_other(finish_y)

    groups = []
    for d in range(0, n, 2):
        groups.append(w_in[d].astype(f32) + pltpu.roll(w_in[d + 1].astype(f32), slots, 1))
    weight = jnp.concatenate(groups, axis=1) * conf_scale
    ys = y_in[...].reshape(n * slots, y_in.shape[2])

    def sparse(v3, target):
        inner = add_pieces(nt(v3, ys))
        coeffs = weight * (1.0 - inner) if target else weight * inner
        return add_pieces(jnp.dot(pieces(coeffs), ys, preferred_element_type=f32))

    residual = sparse(v3, True) + residual
    direction = residual
    norm_now = jnp.sum(residual * residual, axis=1, keepdims=True)
    for sweep in range(ITERS):
        v3 = pieces(direction)
        image = sparse(v3, False) + dense(direction, v3)
        step = norm_now / (jnp.sum(direction * image, axis=1, keepdims=True) + epsilon)
        factors = factors + step * direction
        if sweep + 1 < ITERS:
            residual = residual - step * image
            norm_next = jnp.sum(residual * residual, axis=1, keepdims=True)
            direction = residual + (norm_next / (norm_now + epsilon)) * direction
            norm_now = norm_next
    out[...] = factors

    def sent(to):
        y_copy(to, me).wait_send()
        w_copy(to, me).wait_send()

    each_other(sent)
    in_plane(lambda to: a_copy(to, p).wait_send())
    in_line(lambda to: b_copy(to, z).wait_send(), True)
    if_owner(lambda: in_line(lambda to: c_copy(to, z).wait_send()))
    in_plane(lambda to: d_copy(to, p).wait_send())


def shards(build_factors, nz_build, nz_test, nz_count, start_factors):
    tests, rank = start_factors.shape
    bld_rows = build_factors.shape[0]
    nz_rows = nz_build.shape[0]
    n = lax.axis_size("builds")
    conf_scale = n * bld_rows * tests / (8.0 * nz_rows)
    damping = 0.4 * conf_scale
    slots = tests * MOST
    half = rank // 2
    part = 8
    tiles = 3 * half // part
    line = n // PLANE
    quarter = tiles // PLANE
    owners = max(k for k in range(1, min(line, quarter) + 1) if quarter % k == 0)
    share = quarter // owners
    lump = 16
    chunks = bld_rows // 2048
    lines = n * slots // 128
    dma = pltpu.SemaphoreType.DMA
    return pl.pallas_call(
        functools.partial(kernel, n, owners, conf_scale, damping),
        out_shape=jax.ShapeDtypeStruct((tests, rank), f32),
        in_specs=[pl.BlockSpec(memory_space=pltpu.HBM)] * 5,
        out_specs=pl.BlockSpec(memory_space=pltpu.VMEM),
        scratch_shapes=[
            pltpu.VMEM((1, nz_rows), jnp.int32),
            pltpu.VMEM((1, nz_rows), jnp.int32),
            pltpu.VMEM((1, nz_rows), jnp.int32),
            pltpu.VMEM((tests, rank), f32),
            pltpu.VMEM((bld_rows // lump, lump, rank), bf16),
            pltpu.VMEM((1, nz_rows), jnp.int32),
            pltpu.VMEM((nz_rows, 128), jnp.int32),
            pltpu.VMEM((lines, 128), f32),
            pltpu.VMEM((lines, 128), jnp.int32),
            pltpu.SMEM((lines, 128), jnp.int32),
            pltpu.VMEM((n * slots, lump * lump), bf16),
            pltpu.VMEM((rank, rank), f32),
            pltpu.VMEM((tiles, part, half), f32),
            pltpu.VMEM((PLANE, quarter, part, half), f32),
            pltpu.VMEM((quarter, part, half), f32),
            pltpu.VMEM((line, share, part, half), f32),
            pltpu.VMEM((tiles, part, half), f32),
            pltpu.VMEM((n, slots, rank), bf16),
            pltpu.VMEM((n, slots, rank), bf16),
            pltpu.VMEM((n, tests, 128), bf16),
            pltpu.VMEM((n, tests, 128), bf16),
            dma((chunks,)),
            dma((4,)),
        ]
        + [dma((n,))] * 4
        + [dma((PLANE,))] * 2
        + [dma((line,))] * 4
        + [dma((PLANE,))] * 2,
        compiler_params=pltpu.CompilerParams(
            collective_id=0, has_side_effects=True, vmem_limit_bytes=64 * 1024 * 1024
        ),
    )(
        nz_build[None, :],
        nz_test.reshape(1, nz_rows),
        nz_count[None, :],
        start_factors,
        build_factors.reshape(bld_rows // lump, lump, rank),
    )


def solution(mesh):
    return jax.shard_map(
        shards,
        mesh=mesh,
        in_specs=(
            P("builds", None),
            P(("groups", "builds")),
            P(("groups", "builds"), None),
            P(("groups", "builds")),
            P(("groups", "builds"), None),
        ),
        out_specs=P(("groups", "builds"), None),
        check_vma=False,
    )
```

```python
import functools

import jax
import jax.numpy as jnp
from jax import lax
from jax.experimental import pallas as pl
from jax.experimental.pallas import tpu as pltpu
from jax.sharding import PartitionSpec as P

ITERS = 3
MOST = 4
PLANE = 16
TURN = 4
epsilon = 1e-06
f32 = jnp.float32
bf16 = jnp.bfloat16


def pieces(v):
    high = v.astype(bf16)
    rest = v - high.astype(f32)
    mid = rest.astype(bf16)
    low = (rest - mid.astype(f32)).astype(bf16)
    return jnp.concatenate([high, mid, low], axis=0)


def add_pieces(v):
    rows = v.shape[0] // 3
    return v[:rows] + v[rows : 2 * rows] + v[2 * rows :]


def nt(a, b):
    return lax.dot_general(a, b, (((1,), (1,)), ((), ())), preferred_element_type=f32)


def tn(a, b):
    return lax.dot_general(a, b, (((0,), (0,)), ((), ())), preferred_element_type=f32)


def kernel(
    n, owners, conf_scale, damping,
    nz_hbm, test_hbm, count_hbm, start_hbm, x_hbm, out,
    nz_row, test_row, count_row, start, x_buf, slot, packed, counts_at, at_vmem, at, select, gram,
    tri, plane_in, plane_sum, line_in, tri_sum, y_out, y_in, w_out, w_in,
    x_sem, in_sem, y_send, y_recv, w_send, w_recv,
    a_send, a_recv, b_send, b_recv, c_send, c_recv, d_send, d_recv,
):
    me = lax.axis_index("builds")
    chunks = x_sem.shape[0]
    lumps, lump, rank = x_buf.shape
    chunk = lumps // chunks
    nz = slot.shape[1]
    tests = start.shape[0]
    slots = tests * MOST
    part = tri.shape[1]
    half = tri.shape[2]
    tiles = tri.shape[0]
    line = n // PLANE
    z, p = me // PLANE, lax.rem(me, PLANE)

    small = [
        pltpu.make_async_copy(src, dst, in_sem.at[i])
        for i, (src, dst) in enumerate(
            [(nz_hbm, nz_row), (test_hbm, test_row), (count_hbm, count_row), (start_hbm, start)]
        )
    ]
    for copy in small:
        copy.start()

    def load(c):
        return pltpu.make_async_copy(
            x_hbm.at[pl.ds(c * chunk, chunk)], x_buf.at[pl.ds(c * chunk, chunk)], x_sem.at[c]
        )

    @pl.loop(0, chunks)
    def _(c):
        load(c).start()

    barrier = pltpu.get_barrier_semaphore()

    @pl.loop(1, n)
    def _(j):
        pl.semaphore_signal(
            barrier, inc=1, device_id={"builds": lax.rem(me + j, n)}, device_id_type=pl.DeviceIdType.MESH
        )

    for copy in small:
        copy.wait()

    tests_at = jnp.broadcast_to(test_row[...], (128, nz)).T

    @pl.loop(0, nz // 128)
    def _(c):
        lanes = pl.ds(pl.multiple_of(c * 128, 128), 128)
        ids = test_row[:, lanes]
        first = lax.broadcasted_iota(jnp.int32, (nz, 128), 0)
        second = lax.broadcasted_iota(jnp.int32, (nz, 128), 1) + c * 128
        same = (tests_at == ids) & (first < second)
        earlier = jnp.sum(same.astype(jnp.int32), axis=0, keepdims=True)
        slot[:, lanes] = ids * MOST + earlier

    slot_at = jnp.broadcast_to(slot[...], (128, nz)).T
    packed[...] = jnp.broadcast_to(nz_row[...] * 16 + count_row[...], (128, nz)).T

    @pl.loop(0, n * slots // 128)
    def _(c):
        lane = lax.broadcasted_iota(jnp.int32, (1, 128), 1)
        wanted = lane + c * 128
        held = jnp.sum(jnp.where(slot_at == wanted, packed[...], 0), axis=0, keepdims=True)
        row, amount = held // 16, held % 16
        at_vmem[pl.ds(c, 1), :] = jnp.clip(row // lump, 0, lumps - 1)
        counts_at[pl.ds(c, 1), :] = amount.astype(f32)
        place = jnp.where(amount > 0, (lane % lump) * lump + row % lump, -1)
        place = jnp.broadcast_to(place.astype(f32), (128, 128)).T
        column = lax.broadcasted_iota(jnp.int32, (128, 128), 1).astype(f32)
        both = [(place == column + h * 128.0).astype(f32) for h in range(lump * lump // 128)]
        select[pl.ds(pl.multiple_of(c * 128, 128), 128), :] = jnp.concatenate(both, axis=1).astype(bf16)

    to_scalars = pltpu.make_async_copy(at_vmem, at, in_sem.at[0])
    to_scalars.start()

    def remote(src, dst, send, recv, to):
        return pltpu.make_async_remote_copy(
            src_ref=src, dst_ref=dst, send_sem=send, recv_sem=recv,
            device_id={"builds": to}, device_id_type=pl.DeviceIdType.MESH,
        )

    def y_copy(to, source):
        return remote(y_out.at[to], y_in.at[source], y_send.at[to], y_recv.at[source], to)

    def w_copy(to, source):
        return remote(w_out.at[to], w_in.at[source], w_send.at[to], w_recv.at[source], to)

    pair = 128 // slots

    def block_of(owner):
        line_at, lane_at = owner // pair, lax.rem(owner, pair) * slots
        rows = []
        for b in range(slots // lump):
            near = jnp.concatenate(
                [x_buf[at[line_at, lane_at + b * lump + i]] for i in range(lump)], axis=0
            )
            chosen = select[pl.ds(pl.multiple_of(owner * slots + b * lump, lump), lump), :]
            rows.append(jnp.dot(chosen, near, preferred_element_type=f32).astype(bf16))
        counts = jnp.broadcast_to(counts_at[pl.ds(line_at, 1), :], (tests, 128))
        counts = pltpu.roll(counts, lax.rem(128 - lane_at, 128), 1)
        test = lax.broadcasted_iota(jnp.int32, counts.shape, 0)
        lane = lax.broadcasted_iota(jnp.int32, counts.shape, 1)
        return jnp.concatenate(rows, axis=0), jnp.where(lane // MOST == test, counts, 0.0).astype(bf16)

    gram[...] = jnp.zeros_like(gram)

    def add_gram(c):
        x = x_buf[pl.ds(c * chunk, chunk)].reshape(chunk * lump, rank)
        gram[...] += tn(x, x)

    early = max(chunks * 5 // 12, chunks - (n - 1))
    late = chunks - early

    @pl.loop(0, early)
    def _(c):
        load(c).wait()
        add_gram(c)

    @pl.loop(early, chunks)
    def _(c):
        load(c).wait()

    quarter = tiles // PLANE
    share = quarter // owners

    def in_plane(body):
        for k in range(1, PLANE):
            body(lax.rem(p + k, PLANE))

    def in_line(body, only_owners=False):
        @pl.loop(1, line)
        def _(k):
            other = lax.rem(z + k, line)
            if only_owners and owners < line:
                pl.when(other < owners)(lambda: body(other))
            else:
                body(other)

    def if_owner(body):
        if owners == line:
            body()
        else:
            pl.when(z < owners)(body)

    def a_copy(to, source):
        return remote(
            tri.at[pl.ds(to * quarter, quarter)], plane_in.at[source],
            a_send.at[to], a_recv.at[source], z * PLANE + to,
        )

    def b_copy(to, source):
        return remote(
            plane_sum.at[pl.ds(to * share, share)], line_in.at[source],
            b_send.at[to], b_recv.at[source], to * PLANE + p,
        )

    def c_copy(to, source):
        there = pl.ds(p * quarter + source * share, share)
        return remote(tri_sum.at[there], tri_sum.at[there], c_send.at[to], c_recv.at[source], to * PLANE + p)

    def d_copy(to, source):
        there = pl.ds(source * quarter, quarter)
        return remote(tri_sum.at[there], tri_sum.at[there], d_send.at[to], d_recv.at[source], z * PLANE + to)

    def gather(first, last, with_gram=False):
        @pl.loop(first, last)
        def _(u):
            turn = u // TURN
            away = n // TURN // 2 + ((turn + 1) // 2) * (1 - 2 * lax.rem(turn + 1, 2))
            to = lax.rem(me // TURN + away, n // TURN) * TURN + lax.rem(me + u + 1, TURN)
            rows, counts = block_of(to)
            y_out[to] = rows
            w_out[to] = counts
            y_copy(to, me).start()
            w_copy(to, me).start()
            if with_gram:
                add_gram(early + u)

    pl.semaphore_wait(barrier, n - 1)
    to_scalars.wait()
    gather(0, late, True)

    per = half // part
    for i in range(per):
        tri[i] = gram[i * part : (i + 1) * part, :half]
        tri[per + i] = gram[i * part : (i + 1) * part, half:]
        tri[2 * per + i] = gram[half + i * part : half + (i + 1) * part, half:]

    in_plane(lambda to: a_copy(to, p).start())
    cuts = [late + (n - 1 - late) * i // 4 for i in range(5)]
    gather(cuts[0], cuts[1])

    plane_in[p] = tri[pl.ds(p * quarter, quarter)]
    in_plane(lambda source: a_copy(p, source).wait_recv())
    plane_sum[...] = jnp.sum(plane_in[...], axis=0)
    in_line(lambda to: b_copy(to, z).start(), True)
    gather(cuts[1], cuts[2])

    def reduce():
        line_in[z] = plane_sum[pl.ds(z * share, share)]
        in_line(lambda source: b_copy(z, source).wait_recv())
        tri_sum[pl.ds(p * quarter + z * share, share)] = jnp.sum(line_in[...], axis=0)
        in_line(lambda to: c_copy(to, z).start())

    if_owner(reduce)
    gather(cuts[2], cuts[3])
    in_line(lambda source: c_copy(z, source).wait_recv(), True)
    in_plane(lambda to: d_copy(to, p).start())
    gather(cuts[3], cuts[4])
    rows, counts = block_of(me)
    y_in[me] = rows
    w_in[me] = counts

    in_plane(lambda source: d_copy(p, source).wait_recv())
    full = tri_sum[...].reshape(3 * half, half)
    cross = full[half : 2 * half]
    shared = jnp.concatenate(
        [
            jnp.concatenate([full[:half], cross], axis=1),
            jnp.concatenate([cross.T, full[2 * half :]], axis=1),
        ],
        axis=0,
    )
    shared3 = pieces(shared)

    def dense(v, v3):
        wide = add_pieces(nt(v3, shared3))
        return wide[:, :rank] + wide[:, rank : 2 * rank] + wide[:, 2 * rank :] + damping * v

    factors = start[...]
    v3 = pieces(factors)
    residual = -dense(factors, v3)

    def each_other(body):
        @pl.loop(1, n)
        def _(j):
            body(lax.rem(me + j, n))

    def finish_y(source):
        y_copy(me, source).wait_recv()
        w_copy(me, source).wait_recv()

    each_other(finish_y)

    groups = []
    for d in range(0, n, 2):
        groups.append(w_in[d].astype(f32) + pltpu.roll(w_in[d + 1].astype(f32), slots, 1))
    weight = jnp.concatenate(groups, axis=1) * conf_scale
    ys = y_in[...].reshape(n * slots, y_in.shape[2])

    def sparse(v3, target):
        inner = add_pieces(nt(v3, ys))
        coeffs = weight * (1.0 - inner) if target else weight * inner
        return add_pieces(jnp.dot(pieces(coeffs), ys, preferred_element_type=f32))

    residual = sparse(v3, True) + residual
    direction = residual
    norm_now = jnp.sum(residual * residual, axis=1, keepdims=True)
    for sweep in range(ITERS):
        v3 = pieces(direction)
        image = sparse(v3, False) + dense(direction, v3)
        step = norm_now / (jnp.sum(direction * image, axis=1, keepdims=True) + epsilon)
        factors = factors + step * direction
        if sweep + 1 < ITERS:
            residual = residual - step * image
            norm_next = jnp.sum(residual * residual, axis=1, keepdims=True)
            direction = residual + (norm_next / (norm_now + epsilon)) * direction
            norm_now = norm_next
    out[...] = factors

    def sent(to):
        y_copy(to, me).wait_send()
        w_copy(to, me).wait_send()

    each_other(sent)
    in_plane(lambda to: a_copy(to, p).wait_send())
    in_line(lambda to: b_copy(to, z).wait_send(), True)
    if_owner(lambda: in_line(lambda to: c_copy(to, z).wait_send()))
    in_plane(lambda to: d_copy(to, p).wait_send())


def shards(build_factors, nz_build, nz_test, nz_count, start_factors):
    tests, rank = start_factors.shape
    bld_rows = build_factors.shape[0]
    nz_rows = nz_build.shape[0]
    n = lax.axis_size("builds")
    conf_scale = n * bld_rows * tests / (8.0 * nz_rows)
    damping = 0.4 * conf_scale
    slots = tests * MOST
    half = rank // 2
    part = 8
    tiles = 3 * half // part
    line = n // PLANE
    quarter = tiles // PLANE
    owners = max(k for k in range(1, min(line, quarter) + 1) if quarter % k == 0)
    share = quarter // owners
    lump = 16
    chunks = bld_rows // 2048
    lines = n * slots // 128
    dma = pltpu.SemaphoreType.DMA
    return pl.pallas_call(
        functools.partial(kernel, n, owners, conf_scale, damping),
        out_shape=jax.ShapeDtypeStruct((tests, rank), f32),
        in_specs=[pl.BlockSpec(memory_space=pltpu.HBM)] * 5,
        out_specs=pl.BlockSpec(memory_space=pltpu.VMEM),
        scratch_shapes=[
            pltpu.VMEM((1, nz_rows), jnp.int32),
            pltpu.VMEM((1, nz_rows), jnp.int32),
            pltpu.VMEM((1, nz_rows), jnp.int32),
            pltpu.VMEM((tests, rank), f32),
            pltpu.VMEM((bld_rows // lump, lump, rank), bf16),
            pltpu.VMEM((1, nz_rows), jnp.int32),
            pltpu.VMEM((nz_rows, 128), jnp.int32),
            pltpu.VMEM((lines, 128), f32),
            pltpu.VMEM((lines, 128), jnp.int32),
            pltpu.SMEM((lines, 128), jnp.int32),
            pltpu.VMEM((n * slots, lump * lump), bf16),
            pltpu.VMEM((rank, rank), f32),
            pltpu.VMEM((tiles, part, half), f32),
            pltpu.VMEM((PLANE, quarter, part, half), f32),
            pltpu.VMEM((quarter, part, half), f32),
            pltpu.VMEM((line, share, part, half), f32),
            pltpu.VMEM((tiles, part, half), f32),
            pltpu.VMEM((n, slots, rank), bf16),
            pltpu.VMEM((n, slots, rank), bf16),
            pltpu.VMEM((n, tests, 128), bf16),
            pltpu.VMEM((n, tests, 128), bf16),
            dma((chunks,)),
            dma((4,)),
        ]
        + [dma((n,))] * 4
        + [dma((PLANE,))] * 2
        + [dma((line,))] * 4
        + [dma((PLANE,))] * 2,
        compiler_params=pltpu.CompilerParams(
            collective_id=0, has_side_effects=True, vmem_limit_bytes=64 * 1024 * 1024
        ),
    )(
        nz_build[None, :],
        nz_test.reshape(1, nz_rows),
        nz_count[None, :],
        start_factors,
        build_factors.reshape(bld_rows // lump, lump, rank),
    )


def solution(mesh):
    return jax.shard_map(
        shards,
        mesh=mesh,
        in_specs=(
            P("builds", None),
            P(("groups", "builds")),
            P(("groups", "builds"), None),
            P(("groups", "builds")),
            P(("groups", "builds"), None),
        ),
        out_specs=P(("groups", "builds"), None),
        check_vma=False,
    )
```
